32 devices in a mesh: groups: 2 (over x), tm: 16 (over z, y, core).
Axes of the slice: x: 2, y: 2, z: 4, core: 2. Of those that a mesh axis runs over, the one named last changes fastest.
Arguments:
- samples: float32 [16384, 2048], P('groups', 'tm'), parts along dimension 0, may hold values from -6 to 6
- test_matrix: float32 [4096, 256], P(('groups', 'tm')), parts along dimension 0, may hold values from -0.125 to 0.125
Outputs:
- basis: float32 [16384, 256], P(('groups', 'tm')), parts along dimension 0
- coordinates: float32 [512, 2048], P('groups', 'tm'), parts along dimension 0
The draws below stay inside these ranges and needn't reach their ends.
There are 2 independent parts, one for each index of `groups`. The reference program is written for one: setup_inputs(seed, part) draws one part's arguments, and reference() takes and returns one part's arrays. A program takes and returns all parts, laid end to end along the dimension named above; each array names one. Nothing has to cross between parts.
All inputs are finite; a program needn't handle non-finite values.
Results may differ from the reference program's by a relative error of at most 0.0003.
Values sent between devices are 32-bit elements; how exact they have to be, the bound alone decides.
A program may use at most 64 MiB of HBM per device.

```python
import jax
import jax.numpy as jnp
from jax import lax

C = 8192
K = 256
S = 2048


def with_spikes(array, rng, source, target, parts, factor):
    def block_of(dim):
        return (jnp.arange(array.shape[dim]) // (array.shape[dim] // parts)).reshape((-1,) + (1,) * (array.ndim - 1 - dim))

    first = jax.random.permutation(rng, parts)[block_of(target)]
    far = (block_of(target) + parts // 2) % parts
    return jnp.where((block_of(source) == first) | (block_of(source) == far), factor * array, array)


def steps_of(key, shape, cuts, low, high):
    def one(dim, blocks):
        draws = jax.random.uniform(jax.random.fold_in(jax.random.fold_in(key, 6), dim), (blocks,), jnp.float32, low / len(cuts), high / len(cuts))
        return jnp.repeat(jnp.exp(draws), shape[dim] // blocks).reshape((-1,) + (1,) * (len(shape) - dim - 1))

    gain = one(*cuts[0])
    for cut in cuts[1:]:
        gain = gain * one(*cut)
    return gain


def centred(key, shape, width, most, cuts=(), held_as=jnp.bfloat16):
    drawn = width * jax.random.normal(key, shape, jnp.float32)
    if cuts:
        drawn = drawn * steps_of(key, shape, cuts, -0.22, 0.18)
    return jnp.clip(drawn, -most, most).astype(held_as)


def gaussian_with(key, dims, scale, bound, cuts, heavy, held_as=jnp.bfloat16):
    result = scale * jax.random.normal(key, dims, jnp.float32)
    if cuts:
        result = result * steps_of(key, dims, cuts, -0.22, 0.18)
    return jnp.clip(with_spikes(result, jax.random.fold_in(key, 3), *heavy), -bound, bound).astype(held_as)


def setup_inputs(seed: int = 0, part: int = 0) -> dict:
    keys = jax.random.split(jax.random.key(seed), 3)
    part_keys = jax.random.split(jax.random.fold_in(keys[2], part), 3)
    return {
        "samples": gaussian_with(part_keys[0], (C, S), 1.0, 6.0, ((1, 16),), (1, 0, 16, 2.0), jnp.float32),
        "test_matrix": centred(part_keys[1], (S, K), S ** -0.5, 0.125, ((0, 16),), jnp.float32),
    }


def reference(samples, test_matrix):
    highest = lax.Precision.HIGHEST
    sketch = jnp.dot(samples.astype(jnp.float32), test_matrix.astype(jnp.float32), precision=highest, preferred_element_type=jnp.float32)
    orthonormal, upper = jnp.linalg.qr(sketch)
    signs = jnp.where(jnp.diagonal(upper) < 0, -1.0, 1.0).astype(orthonormal.dtype)
    orthonormal = orthonormal * signs[None, :]
    coordinates = jnp.dot(orthonormal.T.astype(jnp.float32), samples.astype(jnp.float32), precision=highest, preferred_element_type=jnp.float32)
    basis = orthonormal * float(C) ** 0.5
    return (basis, coordinates)
```

```python
import functools

import jax
import jax.numpy as jnp
from jax import lax
from jax.experimental import pallas as pl
from jax.experimental.pallas import tpu as pltpu
from jax.sharding import PartitionSpec as P

HIGHEST = lax.Precision.HIGHEST
PLANE = 4
AHEAD = 4


def exchange_kernel(
    line, parts, sub, a_ref, o_ref, y_out, g_out, p_out,
    abuf, obuf, part, arrived, full, acc, from_core, from_y,
    a_send, a_recv, o_send, o_recv, rs_send, rs_recv, ag_send, ag_recv, fin_send, fin_recv,
):
    width = a_ref.shape[1]
    rank = o_ref.shape[1]
    rows = parts * sub
    me = lax.axis_index("tm")
    z = me // PLANE
    p = me % PLANE
    y, core = p // 2, p % 2
    base = z * PLANE
    place = (p, (1 - y) * 2 + core, y * 2 + 1 - core, (1 - y) * 2 + 1 - core)

    def remote(src, dst, send, recv, target):
        return pltpu.make_async_remote_copy(
            src_ref=src, dst_ref=dst, send_sem=send, recv_sem=recv,
            device_id={"tm": target}, device_id_type=pl.DeviceIdType.MESH,
        )

    def a_copy(d, w, j):
        start = pl.multiple_of((w * PLANE + place[d]) * rows + j * sub, sub)
        return remote(
            a_ref.at[pl.ds(start, sub), :],
            abuf.at[w, pl.ds(pl.multiple_of(j * sub, sub), sub), pl.ds(d * width, width)],
            a_send.at[d - 1, w, j], a_recv.at[d - 1, w, j], base + place[d],
        )

    def o_copy(d):
        return remote(
            o_ref, obuf.at[pl.ds(d * width, width), :], o_send.at[d - 1], o_recv.at[d - 1], base + place[d]
        )

    def at(ref, w, j):
        return ref.at[w, pl.ds(pl.multiple_of(j * sub, sub), sub), :]

    def rs_copy(way, w, j):
        return remote(
            at(part, w, j), arrived.at[way, w, pl.ds(pl.multiple_of(j * sub, sub), sub), :],
            rs_send.at[w, j], rs_recv.at[way, w, j], me + (PLANE if way == 0 else -PLANE),
        )

    def ag_copy(way, w, j):
        return remote(
            at(full, w, j), at(full, w, j),
            ag_send.at[way, w, j], ag_recv.at[w, j], me + (PLANE if way == 0 else -PLANE),
        )

    has_left, has_right = z > 0, z < line - 1
    barrier = pltpu.get_barrier_semaphore()

    def greet(target):
        pl.semaphore_signal(barrier, inc=1, device_id={"tm": target}, device_id_type=pl.DeviceIdType.MESH)

    for d in range(1, PLANE):
        greet(base + place[d])

    @pl.when(has_left)
    def _():
        greet(me - PLANE)

    @pl.when(has_right)
    def _():
        greet(me + PLANE)

    pl.semaphore_wait(barrier, PLANE - 1 + has_left.astype(jnp.int32) + has_right.astype(jnp.int32))

    for d in (1, 3, 2):
        o_copy(d).start()

    def send_a(step):
        t, j = step // parts, step % parts

        def go(w):
            for d in (1, 3, 2):
                a_copy(d, w, j).start()

        @pl.when(line - 1 - t > z)
        def _():
            go(line - 1 - t)

        @pl.when(jnp.logical_and(t < z, t < line - 1))
        def _():
            go(t)

        @pl.when(t == line - 1)
        def _():
            go(z)

    steps = line * parts
    ahead = min(AHEAD, steps)
    for s in range(ahead):
        send_a(jnp.int32(s))

    def keep_own(w, _):
        start = pl.multiple_of((w * PLANE + p) * rows, rows)
        abuf[w, :, pl.ds(0, width)] = a_ref[pl.ds(start, rows), :]
        return 0

    lax.fori_loop(0, line, keep_own, 0)
    obuf[pl.ds(0, width), :] = o_ref[...]
    acc[...] = jnp.zeros_like(acc)
    for d in range(1, PLANE):
        o_copy(d).wait_recv()

    def product(w, j):
        for d in range(1, PLANE):
            a_copy(d, w, j).wait_recv()
        return jnp.dot(at(abuf, w, j)[...], obuf[...], precision=HIGHEST, preferred_element_type=jnp.float32)

    def use(w, j):
        block = at(full, w, j)[...]
        both = jnp.concatenate([block, at(abuf, w, j)[...]], axis=1)
        acc[...] += lax.dot_general(
            block, both, (((0,), (0,)), ((), ())), precision=HIGHEST, preferred_element_type=jnp.float32
        )

    def reduce_step(step, _):
        @pl.when(step + ahead < steps)
        def _():
            send_a(step + ahead)

        t, j = step // parts, step % parts

        def pass_on(way, w, inner):
            at(part, w, j)[...] = product(w, j)

            @pl.when(inner)
            def _():
                rs_copy(way, w, j).wait_recv()
                at(part, w, j)[...] += arrived[way, w, pl.ds(pl.multiple_of(j * sub, sub), sub), :]

            rs_copy(way, w, j).start()

        @pl.when(line - 1 - t > z)
        def _():
            pass_on(0, line - 1 - t, has_left)

        @pl.when(jnp.logical_and(t < z, t < line - 1))
        def _():
            pass_on(1, t, has_right)

        @pl.when(t == line - 1)
        def _():
            at(full, z, j)[...] = product(z, j)

            @pl.when(has_left)
            def _():
                rs_copy(0, z, j).wait_recv()
                at(full, z, j)[...] += arrived[0, z, pl.ds(pl.multiple_of(j * sub, sub), sub), :]

            @pl.when(has_right)
            def _():
                rs_copy(1, z, j).wait_recv()
                at(full, z, j)[...] += arrived[1, z, pl.ds(pl.multiple_of(j * sub, sub), sub), :]
                ag_copy(0, z, j).start()

            @pl.when(has_left)
            def _():
                ag_copy(1, z, j).start()

            use(z, j)

        return 0

    lax.fori_loop(0, steps, reduce_step, 0)
    y_out[...] = full[z]

    def gather_step(step, _):
        t, j = step // parts + 1, step % parts

        @pl.when(t <= z)
        def _():
            w = z - t
            ag_copy(0, w, j).wait_recv()

            @pl.when(has_right)
            def _():
                ag_copy(0, w, j).start()

            use(w, j)

        @pl.when(z + t < line)
        def _():
            w = z + t
            ag_copy(1, w, j).wait_recv()

            @pl.when(has_left)
            def _():
                ag_copy(1, w, j).start()

            use(w, j)

        return 0

    lax.fori_loop(0, (line - 1) * parts, gather_step, 0)

    two = 2 * width
    core_copies = (
        remote(acc.at[:, pl.ds(0, rank)], from_core.at[:, pl.ds(0, rank)],
               fin_send.at[0], fin_recv.at[0], base + place[2]),
        remote(acc.at[:, pl.ds(rank + two, two)], from_core.at[:, pl.ds(rank, two)],
               fin_send.at[1], fin_recv.at[1], base + place[2]),
    )
    for copy in core_copies:
        copy.start()
    for copy in core_copies:
        copy.wait()
    acc[:, pl.ds(0, rank + two)] += from_core[...]
    y_copies = (
        remote(acc.at[:, pl.ds(0, rank)], from_y.at[:, pl.ds(0, rank)],
               fin_send.at[2], fin_recv.at[2], base + place[1]),
        remote(acc.at[:, pl.ds(rank + width, width)], from_y.at[:, pl.ds(rank, width)],
               fin_send.at[3], fin_recv.at[3], base + place[1]),
    )
    for copy in y_copies:
        copy.start()
    for copy in y_copies:
        copy.wait()
    g_out[...] = acc[:, pl.ds(0, rank)] + from_y[:, pl.ds(0, rank)]
    p_out[...] = acc[:, pl.ds(rank, width)] + from_y[:, pl.ds(rank, width)]

    for d in range(1, PLANE):
        o_copy(d).wait_send()

    def drain(step, _):
        w, j = step // parts, step % parts
        for d in range(1, PLANE):
            a_copy(d, w, j).wait_send()

        @pl.when(w != z)
        def _():
            rs_copy(0, w, j).wait_send()

        @pl.when(jnp.logical_and(has_right, w <= z))
        def _():
            ag_copy(0, w, j).wait_send()

        @pl.when(jnp.logical_and(has_left, w >= z))
        def _():
            ag_copy(1, w, j).wait_send()

        return 0

    lax.fori_loop(0, steps, drain, 0)


def exchange(n, samples, test_matrix):
    channels, width = samples.shape
    rank = test_matrix.shape[1]
    line = n // PLANE
    rows = channels // n
    sub = min(128, rows)
    parts = rows // sub
    f32 = jnp.float32
    dma = pltpu.SemaphoreType.DMA
    vmem = pl.BlockSpec(memory_space=pltpu.VMEM)
    return pl.pallas_call(
        functools.partial(exchange_kernel, line, parts, sub),
        out_shape=(
            jax.ShapeDtypeStruct((rows, rank), f32),
            jax.ShapeDtypeStruct((rank, rank), f32),
            jax.ShapeDtypeStruct((rank, width), f32),
        ),
        in_specs=[vmem] * 2,
        out_specs=(vmem,) * 3,
        scratch_shapes=[
            pltpu.VMEM((line, rows, PLANE * width), f32),
            pltpu.VMEM((PLANE * width, rank), f32),
            pltpu.VMEM((line, rows, rank), f32),
            pltpu.VMEM((2, line, rows, rank), f32),
            pltpu.VMEM((line, rows, rank), f32),
            pltpu.VMEM((rank, rank + PLANE * width), f32),
            pltpu.VMEM((rank, rank + 2 * width), f32),
            pltpu.VMEM((rank, rank + width), f32),
            dma((PLANE - 1, line, parts)),
            dma((PLANE - 1, line, parts)),
            dma((PLANE - 1,)),
            dma((PLANE - 1,)),
            dma((line, parts)),
            dma((2, line, parts)),
            dma((2, line, parts)),
            dma((line, parts)),
            dma((4,)),
            dma((4,)),
        ],
        compiler_params=pltpu.CompilerParams(
            collective_id=0, has_side_effects=True, vmem_limit_bytes=40 * 1024 * 1024
        ),
    )(samples, test_matrix)


def local(n, samples, test_matrix):
    channels = samples.shape[0]
    sketch, gram, projected = exchange(n, samples, test_matrix)
    factor = jnp.linalg.cholesky(gram)
    orthonormal = jax.scipy.linalg.solve_triangular(factor, sketch.T, lower=True).T
    coordinates = jax.scipy.linalg.solve_triangular(factor, projected, lower=True)
    return (orthonormal * float(channels) ** 0.5, coordinates)


def solution(mesh):
    placed = (P("groups", "tm"), P(("groups", "tm"), None))
    return jax.shard_map(
        functools.partial(local, mesh.shape["tm"]),
        mesh=mesh,
        in_specs=placed,
        out_specs=(P(("groups", "tm"), None), P("groups", "tm")),
        check_vma=False,
    )
```

```python
import functools

import jax
import jax.numpy as jnp
from jax import lax
from jax.experimental import pallas as pl
from jax.experimental.pallas import tpu as pltpu
from jax.sharding import PartitionSpec as P

HIGHEST = lax.Precision.HIGHEST
PLANE = 4
AHEAD = 4


def exchange_kernel(
    line, parts, sub, a_ref, o_ref, y_out, g_out, p_out,
    abuf, obuf, part, arrived, full, acc, from_core, from_y,
    a_send, a_recv, o_send, o_recv, rs_send, rs_recv, ag_send, ag_recv, fin_send, fin_recv,
):
    width = a_ref.shape[1]
    rank = o_ref.shape[1]
    rows = parts * sub
    me = lax.axis_index("tm")
    z = me // PLANE
    p = me % PLANE
    y, core = p // 2, p % 2
    base = z * PLANE
    place = (p, (1 - y) * 2 + core, y * 2 + 1 - core, (1 - y) * 2 + 1 - core)

    def remote(src, dst, send, recv, target):
        return pltpu.make_async_remote_copy(
            src_ref=src, dst_ref=dst, send_sem=send, recv_sem=recv,
            device_id={"tm": target}, device_id_type=pl.DeviceIdType.MESH,
        )

    def a_copy(d, w, j):
        start = pl.multiple_of((w * PLANE + place[d]) * rows + j * sub, sub)
        return remote(
            a_ref.at[pl.ds(start, sub), :],
            abuf.at[w, pl.ds(pl.multiple_of(j * sub, sub), sub), pl.ds(d * width, width)],
            a_send.at[d - 1, w, j], a_recv.at[d - 1, w, j], base + place[d],
        )

    def o_copy(d):
        return remote(
            o_ref, obuf.at[pl.ds(d * width, width), :], o_send.at[d - 1], o_recv.at[d - 1], base + place[d]
        )

    def at(ref, w, j):
        return ref.at[w, pl.ds(pl.multiple_of(j * sub, sub), sub), :]

    def rs_copy(way, w, j):
        return remote(
            at(part, w, j), arrived.at[way, w, pl.ds(pl.multiple_of(j * sub, sub), sub), :],
            rs_send.at[w, j], rs_recv.at[way, w, j], me + (PLANE if way == 0 else -PLANE),
        )

    def ag_copy(way, w, j):
        return remote(
            at(full, w, j), at(full, w, j),
            ag_send.at[way, w, j], ag_recv.at[w, j], me + (PLANE if way == 0 else -PLANE),
        )

    has_left, has_right = z > 0, z < line - 1
    barrier = pltpu.get_barrier_semaphore()

    def greet(target):
        pl.semaphore_signal(barrier, inc=1, device_id={"tm": target}, device_id_type=pl.DeviceIdType.MESH)

    for d in range(1, PLANE):
        greet(base + place[d])

    @pl.when(has_left)
    def _():
        greet(me - PLANE)

    @pl.when(has_right)
    def _():
        greet(me + PLANE)

    pl.semaphore_wait(barrier, PLANE - 1 + has_left.astype(jnp.int32) + has_right.astype(jnp.int32))

    for d in (1, 3, 2):
        o_copy(d).start()

    def send_a(step):
        t, j = step // parts, step % parts

        def go(w):
            for d in (1, 3, 2):
                a_copy(d, w, j).start()

        @pl.when(line - 1 - t > z)
        def _():
            go(line - 1 - t)

        @pl.when(jnp.logical_and(t < z, t < line - 1))
        def _():
            go(t)

        @pl.when(t == line - 1)
        def _():
            go(z)

    steps = line * parts
    ahead = min(AHEAD, steps)
    for s in range(ahead):
        send_a(jnp.int32(s))

    def keep_own(w, _):
        start = pl.multiple_of((w * PLANE + p) * rows, rows)
        abuf[w, :, pl.ds(0, width)] = a_ref[pl.ds(start, rows), :]
        return 0

    lax.fori_loop(0, line, keep_own, 0)
    obuf[pl.ds(0, width), :] = o_ref[...]
    acc[...] = jnp.zeros_like(acc)
    for d in range(1, PLANE):
        o_copy(d).wait_recv()

    def product(w, j):
        for d in range(1, PLANE):
            a_copy(d, w, j).wait_recv()
        return jnp.dot(at(abuf, w, j)[...], obuf[...], precision=HIGHEST, preferred_element_type=jnp.float32)

    def use(w, j):
        block = at(full, w, j)[...]
        both = jnp.concatenate([block, at(abuf, w, j)[...]], axis=1)
        acc[...] += lax.dot_general(
            block, both, (((0,), (0,)), ((), ())), precision=HIGHEST, preferred_element_type=jnp.float32
        )

    def reduce_step(step, _):
        @pl.when(step + ahead < steps)
        def _():
            send_a(step + ahead)

        t, j = step // parts, step % parts

        def pass_on(way, w, inner):
            at(part, w, j)[...] = product(w, j)

            @pl.when(inner)
            def _():
                rs_copy(way, w, j).wait_recv()
                at(part, w, j)[...] += arrived[way, w, pl.ds(pl.multiple_of(j * sub, sub), sub), :]

            rs_copy(way, w, j).start()

        @pl.when(line - 1 - t > z)
        def _():
            pass_on(0, line - 1 - t, has_left)

        @pl.when(jnp.logical_and(t < z, t < line - 1))
        def _():
            pass_on(1, t, has_right)

        @pl.when(t == line - 1)
        def _():
            at(full, z, j)[...] = product(z, j)

            @pl.when(has_left)
            def _():
                rs_copy(0, z, j).wait_recv()
                at(full, z, j)[...] += arrived[0, z, pl.ds(pl.multiple_of(j * sub, sub), sub), :]

            @pl.when(has_right)
            def _():
                rs_copy(1, z, j).wait_recv()
                at(full, z, j)[...] += arrived[1, z, pl.ds(pl.multiple_of(j * sub, sub), sub), :]
                ag_copy(0, z, j).start()

            @pl.when(has_left)
            def _():
                ag_copy(1, z, j).start()

            use(z, j)

        return 0

    lax.fori_loop(0, steps, reduce_step, 0)
    y_out[...] = full[z]

    def gather_step(step, _):
        t, j = step // parts + 1, step % parts

        @pl.when(t <= z)
        def _():
            w = z - t
            ag_copy(0, w, j).wait_recv()

            @pl.when(has_right)
            def _():
                ag_copy(0, w, j).start()

            use(w, j)

        @pl.when(z + t < line)
        def _():
            w = z + t
            ag_copy(1, w, j).wait_recv()

            @pl.when(has_left)
            def _():
                ag_copy(1, w, j).start()

            use(w, j)

        return 0

    lax.fori_loop(0, (line - 1) * parts, gather_step, 0)

    two = 2 * width
    core_copies = (
        remote(acc.at[:, pl.ds(0, rank)], from_core.at[:, pl.ds(0, rank)],
               fin_send.at[0], fin_recv.at[0], base + place[2]),
        remote(acc.at[:, pl.ds(rank + two, two)], from_core.at[:, pl.ds(rank, two)],
               fin_send.at[1], fin_recv.at[1], base + place[2]),
    )
    for copy in core_copies:
        copy.start()
    for copy in core_copies:
        copy.wait()
    acc[:, pl.ds(0, rank + two)] += from_core[...]
    y_copies = (
        remote(acc.at[:, pl.ds(0, rank)], from_y.at[:, pl.ds(0, rank)],
               fin_send.at[2], fin_recv.at[2], base + place[1]),
        remote(acc.at[:, pl.ds(rank + width, width)], from_y.at[:, pl.ds(rank, width)],
               fin_send.at[3], fin_recv.at[3], base + place[1]),
    )
    for copy in y_copies:
        copy.start()
    for copy in y_copies:
        copy.wait()
    g_out[...] = acc[:, pl.ds(0, rank)] + from_y[:, pl.ds(0, rank)]
    p_out[...] = acc[:, pl.ds(rank, width)] + from_y[:, pl.ds(rank, width)]

    for d in range(1, PLANE):
        o_copy(d).wait_send()

    def drain(step, _):
        w, j = step // parts, step % parts
        for d in range(1, PLANE):
            a_copy(d, w, j).wait_send()

        @pl.when(w != z)
        def _():
            rs_copy(0, w, j).wait_send()

        @pl.when(jnp.logical_and(has_right, w <= z))
        def _():
            ag_copy(0, w, j).wait_send()

        @pl.when(jnp.logical_and(has_left, w >= z))
        def _():
            ag_copy(1, w, j).wait_send()

        return 0

    lax.fori_loop(0, steps, drain, 0)


def exchange(n, samples, test_matrix):
    channels, width = samples.shape
    rank = test_matrix.shape[1]
    line = n // PLANE
    rows = channels // n
    sub = min(128, rows)
    parts = rows // sub
    f32 = jnp.float32
    dma = pltpu.SemaphoreType.DMA
    vmem = pl.BlockSpec(memory_space=pltpu.VMEM)
    return pl.pallas_call(
        functools.partial(exchange_kernel, line, parts, sub),
        out_shape=(
            jax.ShapeDtypeStruct((rows, rank), f32),
            jax.ShapeDtypeStruct((rank, rank), f32),
            jax.ShapeDtypeStruct((rank, width), f32),
        ),
        in_specs=[vmem] * 2,
        out_specs=(vmem,) * 3,
        scratch_shapes=[
            pltpu.VMEM((line, rows, PLANE * width), f32),
            pltpu.VMEM((PLANE * width, rank), f32),
            pltpu.VMEM((line, rows, rank), f32),
            pltpu.VMEM((2, line, rows, rank), f32),
            pltpu.VMEM((line, rows, rank), f32),
            pltpu.VMEM((rank, rank + PLANE * width), f32),
            pltpu.VMEM((rank, rank + 2 * width), f32),
            pltpu.VMEM((rank, rank + width), f32),
            dma((PLANE - 1, line, parts)),
            dma((PLANE - 1, line, parts)),
            dma((PLANE - 1,)),
            dma((PLANE - 1,)),
            dma((line, parts)),
            dma((2, line, parts)),
            dma((2, line, parts)),
            dma((line, parts)),
            dma((4,)),
            dma((4,)),
        ],
        compiler_params=pltpu.CompilerParams(
            collective_id=0, has_side_effects=True, vmem_limit_bytes=40 * 1024 * 1024
        ),
    )(samples, test_matrix)


def dot(a, b, contract=(1, 0)):
    return lax.dot_general(
        a, b, (((contract[0],), (contract[1],)), ((), ())), precision=HIGHEST, preferred_element_type=jnp.float32
    )


def inverse_factor(gram):
    n = gram.shape[0]
    blocks = n // 8
    row = lax.broadcasted_iota(jnp.int32, (8, n), 0)
    lane = lax.broadcasted_iota(jnp.int32, (8, n), 1)
    left = [gram[8 * i : 8 * i + 8, :] for i in range(blocks)]
    right = [jnp.where(lane == row + 8 * i, 1.0, 0.0) for i in range(blocks)]

    def spread(block, j):
        return jnp.broadcast_to(block[j : j + 1, :], (8, n))

    done = []
    for g in range(blocks):
        cols = {
            i: [jnp.broadcast_to(left[i][:, 8 * g + j : 8 * g + j + 1], (8, n)) for j in range(8)]
            for i in range(g, blocks)
        }
        scale = jnp.zeros((8, n), jnp.float32)
        for j in range(8):
            pivot = spread(cols[g][j], j)
            inverse = 1.0 / pivot
            scale = jnp.where(row == j, lax.rsqrt(pivot), scale)
            across = [spread(cols[g][j], l) for l in range(8)]
            left_row, right_row = spread(left[g], j), spread(right[g], j)
            for i in range(g, blocks):
                times = cols[i][j] * inverse
                if i == g:
                    times = jnp.where(row > j, times, 0.0)
                for l in range(j + 1, 8):
                    cols[i][l] = cols[i][l] - times * across[l]
                left[i] = left[i] - times * left_row
                right[i] = right[i] - times * right_row
        done.append(right[g] * scale)
    return jnp.concatenate(done, axis=0)


def inverse_of(gram):
    rank = gram.shape[0]
    if rank <= 128:
        return inverse_factor(gram)
    half = rank // 2
    first = inverse_of(gram[:half, :half])
    lower = dot(gram[half:, :half], first, (1, 1))
    second = inverse_of(gram[half:, half:] - dot(lower, lower, (1, 1)))
    corner = -dot(second, dot(lower, first))
    top = jnp.concatenate([first, jnp.zeros_like(first)], axis=1)
    return jnp.concatenate([top, jnp.concatenate([corner, second], axis=1)], axis=0)


def factor_kernel(root, y_ref, g_ref, p_ref, basis_ref, coordinates_ref):
    inverse = inverse_of(g_ref[...])
    basis_ref[...] = dot(y_ref[...], inverse, (1, 1)) * root
    coordinates_ref[...] = dot(inverse, p_ref[...])


def local(n, samples, test_matrix):
    channels = samples.shape[0]
    sketch, gram, projected = exchange(n, samples, test_matrix)
    vmem = pl.BlockSpec(memory_space=pltpu.VMEM)
    return pl.pallas_call(
        functools.partial(factor_kernel, float(channels) ** 0.5),
        out_shape=(
            jax.ShapeDtypeStruct(sketch.shape, jnp.float32),
            jax.ShapeDtypeStruct(projected.shape, jnp.float32),
        ),
        in_specs=[vmem] * 3,
        out_specs=(vmem,) * 2,
        compiler_params=pltpu.CompilerParams(vmem_limit_bytes=16 * 1024 * 1024),
    )(sketch, gram, projected)


def solution(mesh):
    placed = (P("groups", "tm"), P(("groups", "tm"), None))
    return jax.shard_map(
        functools.partial(local, mesh.shape["tm"]),
        mesh=mesh,
        in_specs=placed,
        out_specs=(P(("groups", "tm"), None), P("groups", "tm")),
        check_vma=False,
    )
```

```python
import functools

import jax
import jax.numpy as jnp
from jax import lax
from jax.experimental import pallas as pl
from jax.experimental.pallas import tpu as pltpu
from jax.sharding import PartitionSpec as P

HIGHEST = lax.Precision.HIGHEST
PLANE = 4
AHEAD = 16


def exchange_kernel(
    line, parts, sub, a_ref, o_ref, y_out, g_out, p_out,
    abuf, obuf, part, arrived, full, acc, from_core, from_y,
    a_send, a_recv, o_send, o_recv, rs_send, rs_recv, ag_send, ag_recv, fin_send, fin_recv,
):
    width = a_ref.shape[1]
    rank = o_ref.shape[1]
    rows = parts * sub
    me = lax.axis_index("tm")
    z = me // PLANE
    p = me % PLANE
    y, core = p // 2, p % 2
    base = z * PLANE
    place = (p, (1 - y) * 2 + core, y * 2 + 1 - core, (1 - y) * 2 + 1 - core)

    def remote(src, dst, send, recv, target):
        return pltpu.make_async_remote_copy(
            src_ref=src, dst_ref=dst, send_sem=send, recv_sem=recv,
            device_id={"tm": target}, device_id_type=pl.DeviceIdType.MESH,
        )

    def a_copy(d, w, j):
        start = pl.multiple_of((w * PLANE + place[d]) * rows + j * sub, sub)
        return remote(
            a_ref.at[pl.ds(start, sub), :],
            abuf.at[w, pl.ds(pl.multiple_of(j * sub, sub), sub), pl.ds(d * width, width)],
            a_send.at[d - 1, w, j], a_recv.at[d - 1, w, j], base + place[d],
        )

    def o_copy(d):
        return remote(
            o_ref, obuf.at[pl.ds(d * width, width), :], o_send.at[d - 1], o_recv.at[d - 1], base + place[d]
        )

    def at(ref, w, j):
        return ref.at[w, pl.ds(pl.multiple_of(j * sub, sub), sub), :]

    def rs_copy(way, w, j):
        return remote(
            at(part, w, j), arrived.at[way, w, pl.ds(pl.multiple_of(j * sub, sub), sub), :],
            rs_send.at[w, j], rs_recv.at[way, w, j], me + (PLANE if way == 0 else -PLANE),
        )

    def ag_copy(way, w, j):
        return remote(
            at(full, w, j), at(full, w, j),
            ag_send.at[way, w, j], ag_recv.at[w, j], me + (PLANE if way == 0 else -PLANE),
        )

    has_left, has_right = z > 0, z < line - 1
    barrier = pltpu.get_barrier_semaphore()

    def greet(target):
        pl.semaphore_signal(barrier, inc=1, device_id={"tm": target}, device_id_type=pl.DeviceIdType.MESH)

    for d in range(1, PLANE):
        greet(base + place[d])

    @pl.when(has_left)
    def _():
        greet(me - PLANE)

    @pl.when(has_right)
    def _():
        greet(me + PLANE)

    pl.semaphore_wait(barrier, PLANE - 1 + has_left.astype(jnp.int32) + has_right.astype(jnp.int32))

    for d in (1, 3, 2):
        o_copy(d).start()

    def send_a(step):
        t, j = step // parts, step % parts

        def go(w):
            for d in (1, 3, 2):
                a_copy(d, w, j).start()

        @pl.when(line - 1 - t > z)
        def _():
            go(line - 1 - t)

        @pl.when(jnp.logical_and(t < z, t < line - 1))
        def _():
            go(t)

        @pl.when(t == line - 1)
        def _():
            go(z)

    steps = line * parts
    ahead = min(AHEAD, steps)
    for s in range(ahead):
        send_a(jnp.int32(s))

    def keep_own(w, _):
        start = pl.multiple_of((w * PLANE + p) * rows, rows)
        abuf[w, :, pl.ds(0, width)] = a_ref[pl.ds(start, rows), :]
        return 0

    lax.fori_loop(0, line, keep_own, 0)
    obuf[pl.ds(0, width), :] = o_ref[...]
    acc[...] = jnp.zeros_like(acc)
    for d in range(1, PLANE):
        o_copy(d).wait_recv()

    def product(w, j):
        for d in range(1, PLANE):
            a_copy(d, w, j).wait_recv()
        return jnp.dot(at(abuf, w, j)[...], obuf[...], precision=HIGHEST, preferred_element_type=jnp.float32)

    def use(w, j):
        block = at(full, w, j)[...]
        both = jnp.concatenate([block, at(abuf, w, j)[...]], axis=1)
        acc[...] += lax.dot_general(
            block, both, (((0,), (0,)), ((), ())), precision=HIGHEST, preferred_element_type=jnp.float32
        )

    def reduce_step(step, _):
        @pl.when(step + ahead < steps)
        def _():
            send_a(step + ahead)

        t, j = step // parts, step % parts

        def pass_on(way, w, inner):
            at(part, w, j)[...] = product(w, j)

            @pl.when(inner)
            def _():
                rs_copy(way, w, j).wait_recv()
                at(part, w, j)[...] += arrived[way, w, pl.ds(pl.multiple_of(j * sub, sub), sub), :]

            rs_copy(way, w, j).start()

        to_right = line - 1 - t > z

        @pl.when(jnp.logical_and(to_right, z < line // 2))
        def _():
            pass_on(0, line - 1 - t, has_left)

        @pl.when(jnp.logical_and(t < z, t < line - 1))
        def _():
            pass_on(1, t, has_right)

        @pl.when(jnp.logical_and(to_right, z >= line // 2))
        def _():
            pass_on(0, line - 1 - t, has_left)

        @pl.when(t == line - 1)
        def _():
            at(full, z, j)[...] = product(z, j)

            @pl.when(has_left)
            def _():
                rs_copy(0, z, j).wait_recv()
                at(full, z, j)[...] += arrived[0, z, pl.ds(pl.multiple_of(j * sub, sub), sub), :]

            @pl.when(has_right)
            def _():
                rs_copy(1, z, j).wait_recv()
                at(full, z, j)[...] += arrived[1, z, pl.ds(pl.multiple_of(j * sub, sub), sub), :]
                ag_copy(0, z, j).start()

            @pl.when(has_left)
            def _():
                ag_copy(1, z, j).start()

            use(z, j)

        return 0

    lax.fori_loop(0, steps, reduce_step, 0)
    y_out[...] = full[z]

    def gather_step(step, _):
        t, j = step // parts + 1, step % parts

        @pl.when(t <= z)
        def _():
            w = z - t
            ag_copy(0, w, j).wait_recv()

            @pl.when(has_right)
            def _():
                ag_copy(0, w, j).start()

            use(w, j)

        @pl.when(z + t < line)
        def _():
            w = z + t
            ag_copy(1, w, j).wait_recv()

            @pl.when(has_left)
            def _():
                ag_copy(1, w, j).start()

            use(w, j)

        return 0

    lax.fori_loop(0, (line - 1) * parts, gather_step, 0)

    two = 2 * width
    core_copies = (
        remote(acc.at[:, pl.ds(0, rank)], from_core.at[:, pl.ds(0, rank)],
               fin_send.at[0], fin_recv.at[0], base + place[2]),
        remote(acc.at[:, pl.ds(rank + two, two)], from_core.at[:, pl.ds(rank, two)],
               fin_send.at[1], fin_recv.at[1], base + place[2]),
    )
    for copy in core_copies:
        copy.start()
    for copy in core_copies:
        copy.wait()
    acc[:, pl.ds(0, rank + two)] += from_core[...]
    y_copies = (
        remote(acc.at[:, pl.ds(0, rank)], from_y.at[:, pl.ds(0, rank)],
               fin_send.at[2], fin_recv.at[2], base + place[1]),
        remote(acc.at[:, pl.ds(rank + width, width)], from_y.at[:, pl.ds(rank, width)],
               fin_send.at[3], fin_recv.at[3], base + place[1]),
    )
    for copy in y_copies:
        copy.start()
    for copy in y_copies:
        copy.wait()
    g_out[...] = acc[:, pl.ds(0, rank)] + from_y[:, pl.ds(0, rank)]
    p_out[...] = acc[:, pl.ds(rank, width)] + from_y[:, pl.ds(rank, width)]

    for d in range(1, PLANE):
        o_copy(d).wait_send()

    def drain(step, _):
        w, j = step // parts, step % parts
        for d in range(1, PLANE):
            a_copy(d, w, j).wait_send()

        @pl.when(w != z)
        def _():
            rs_copy(0, w, j).wait_send()

        @pl.when(jnp.logical_and(has_right, w <= z))
        def _():
            ag_copy(0, w, j).wait_send()

        @pl.when(jnp.logical_and(has_left, w >= z))
        def _():
            ag_copy(1, w, j).wait_send()

        return 0

    lax.fori_loop(0, steps, drain, 0)


def exchange(n, samples, test_matrix):
    channels, width = samples.shape
    rank = test_matrix.shape[1]
    line = n // PLANE
    rows = channels // n
    sub = min(128, rows)
    parts = rows // sub
    f32 = jnp.float32
    dma = pltpu.SemaphoreType.DMA
    vmem = pl.BlockSpec(memory_space=pltpu.VMEM)
    return pl.pallas_call(
        functools.partial(exchange_kernel, line, parts, sub),
        out_shape=(
            jax.ShapeDtypeStruct((rows, rank), f32),
            jax.ShapeDtypeStruct((rank, rank), f32),
            jax.ShapeDtypeStruct((rank, width), f32),
        ),
        in_specs=[vmem] * 2,
        out_specs=(vmem,) * 3,
        scratch_shapes=[
            pltpu.VMEM((line, rows, PLANE * width), f32),
            pltpu.VMEM((PLANE * width, rank), f32),
            pltpu.VMEM((line, rows, rank), f32),
            pltpu.VMEM((2, line, rows, rank), f32),
            pltpu.VMEM((line, rows, rank), f32),
            pltpu.VMEM((rank, rank + PLANE * width), f32),
            pltpu.VMEM((rank, rank + 2 * width), f32),
            pltpu.VMEM((rank, rank + width), f32),
            dma((PLANE - 1, line, parts)),
            dma((PLANE - 1, line, parts)),
            dma((PLANE - 1,)),
            dma((PLANE - 1,)),
            dma((line, parts)),
            dma((2, line, parts)),
            dma((2, line, parts)),
            dma((line, parts)),
            dma((4,)),
            dma((4,)),
        ],
        compiler_params=pltpu.CompilerParams(
            collective_id=0, has_side_effects=True, vmem_limit_bytes=40 * 1024 * 1024
        ),
    )(samples, test_matrix)


def dot(a, b, contract=(1, 0)):
    return lax.dot_general(
        a, b, (((contract[0],), (contract[1],)), ((), ())), precision=HIGHEST, preferred_element_type=jnp.float32
    )


def inverse_factor(gram):
    n = gram.shape[0]
    blocks = n // 8
    row = lax.broadcasted_iota(jnp.int32, (8, n), 0)
    lane = lax.broadcasted_iota(jnp.int32, (8, n), 1)
    left = [gram[8 * i : 8 * i + 8, :] for i in range(blocks)]
    right = [jnp.where(lane == row + 8 * i, 1.0, 0.0) for i in range(blocks)]

    def spread(block, j):
        return jnp.broadcast_to(block[j : j + 1, :], (8, n))

    done = []
    for g in range(blocks):
        cols = {
            i: [jnp.broadcast_to(left[i][:, 8 * g + j : 8 * g + j + 1], (8, n)) for j in range(8)]
            for i in range(g, blocks)
        }
        scale = jnp.zeros((8, n), jnp.float32)
        for j in range(8):
            pivot = spread(cols[g][j], j)
            inverse = 1.0 / pivot
            scale = jnp.where(row == j, lax.rsqrt(pivot), scale)
            across = [spread(cols[g][j], l) for l in range(8)]
            left_row, right_row = spread(left[g], j), spread(right[g], j)
            for i in range(g, blocks):
                times = cols[i][j] * inverse
                if i == g:
                    times = jnp.where(row > j, times, 0.0)
                for l in range(j + 1, 8):
                    cols[i][l] = cols[i][l] - times * across[l]
                left[i] = left[i] - times * left_row
                right[i] = right[i] - times * right_row
        done.append(right[g] * scale)
    return jnp.concatenate(done, axis=0)


def inverse_of(gram):
    rank = gram.shape[0]
    if rank <= 128:
        return inverse_factor(gram)
    half = rank // 2
    first = inverse_of(gram[:half, :half])
    lower = dot(gram[half:, :half], first, (1, 1))
    second = inverse_of(gram[half:, half:] - dot(lower, lower, (1, 1)))
    corner = -dot(second, dot(lower, first))
    top = jnp.concatenate([first, jnp.zeros_like(first)], axis=1)
    return jnp.concatenate([top, jnp.concatenate([corner, second], axis=1)], axis=0)


def factor_kernel(root, y_ref, g_ref, p_ref, basis_ref, coordinates_ref):
    inverse = inverse_of(g_ref[...])
    basis_ref[...] = dot(y_ref[...], inverse, (1, 1)) * root
    coordinates_ref[...] = dot(inverse, p_ref[...])


def local(n, samples, test_matrix):
    channels = samples.shape[0]
    sketch, gram, projected = exchange(n, samples, test_matrix)
    vmem = pl.BlockSpec(memory_space=pltpu.VMEM)
    return pl.pallas_call(
        functools.partial(factor_kernel, float(channels) ** 0.5),
        out_shape=(
            jax.ShapeDtypeStruct(sketch.shape, jnp.float32),
            jax.ShapeDtypeStruct(projected.shape, jnp.float32),
        ),
        in_specs=[vmem] * 3,
        out_specs=(vmem,) * 2,
        compiler_params=pltpu.CompilerParams(vmem_limit_bytes=16 * 1024 * 1024),
    )(sketch, gram, projected)


def solution(mesh):
    placed = (P("groups", "tm"), P(("groups", "tm"), None))
    return jax.shard_map(
        functools.partial(local, mesh.shape["tm"]),
        mesh=mesh,
        in_specs=placed,
        out_specs=(P(("groups", "tm"), None), P("groups", "tm")),
        check_vma=False,
    )
```

```python
import functools

import jax
import jax.numpy as jnp
from jax import lax
from jax.experimental import pallas as pl
from jax.experimental.pallas import tpu as pltpu
from jax.sharding import PartitionSpec as P

HIGHEST = lax.Precision.HIGHEST
PLANE = 4
AHEAD = 16


def exchange_kernel(
    line, parts, sub, a_ref, o_ref, y_out, g_out, p_out,
    abuf, obuf, part, arrived, full, acc, from_core, from_y,
    a_send, a_recv, o_send, o_recv, rs_send, rs_recv, ag_send, ag_recv, fin_send, fin_recv,
):
    width = a_ref.shape[1]
    rank = o_ref.shape[1]
    rows = parts * sub
    me = lax.axis_index("tm")
    z = me // PLANE
    p = me % PLANE
    y, core = p // 2, p % 2
    base = z * PLANE
    place = (p, (1 - y) * 2 + core, y * 2 + 1 - core, (1 - y) * 2 + 1 - core)

    def remote(src, dst, send, recv, target):
        return pltpu.make_async_remote_copy(
            src_ref=src, dst_ref=dst, send_sem=send, recv_sem=recv,
            device_id={"tm": target}, device_id_type=pl.DeviceIdType.MESH,
        )

    def a_copy(d, w, j):
        start = pl.multiple_of((w * PLANE + place[d]) * rows + j * sub, sub)
        return remote(
            a_ref.at[pl.ds(start, sub), :],
            abuf.at[w, pl.ds(pl.multiple_of(j * sub, sub), sub), pl.ds(d * width, width)],
            a_send.at[d - 1, w, j], a_recv.at[d - 1, w, j], base + place[d],
        )

    def o_copy(d):
        return remote(
            o_ref, obuf.at[pl.ds(d * width, width), :], o_send.at[d - 1], o_recv.at[d - 1], base + place[d]
        )

    def at(ref, w, j):
        return ref.at[w, pl.ds(pl.multiple_of(j * sub, sub), sub), :]

    def rs_copy(way, w, j):
        return remote(
            at(part, w, j), arrived.at[way, w, pl.ds(pl.multiple_of(j * sub, sub), sub), :],
            rs_send.at[w, j], rs_recv.at[way, w, j], me + (PLANE if way == 0 else -PLANE),
        )

    def ag_copy(way, w, j):
        return remote(
            at(full, w, j), at(full, w, j),
            ag_send.at[way, w, j], ag_recv.at[w, j], me + (PLANE if way == 0 else -PLANE),
        )

    has_left, has_right = z > 0, z < line - 1
    barrier = pltpu.get_barrier_semaphore()

    def greet(target):
        pl.semaphore_signal(barrier, inc=1, device_id={"tm": target}, device_id_type=pl.DeviceIdType.MESH)

    for d in range(1, PLANE):
        greet(base + place[d])

    @pl.when(has_left)
    def _():
        greet(me - PLANE)

    @pl.when(has_right)
    def _():
        greet(me + PLANE)

    pl.semaphore_wait(barrier, PLANE - 1 + has_left.astype(jnp.int32) + has_right.astype(jnp.int32))

    for d in (1, 3, 2):
        o_copy(d).start()

    def send_a(step):
        t, j = step // parts, step % parts

        def go(w):
            for d in (1, 3, 2):
                a_copy(d, w, j).start()

        @pl.when(line - 1 - t > z)
        def _():
            go(line - 1 - t)

        @pl.when(jnp.logical_and(t < z, t < line - 1))
        def _():
            go(t)

        @pl.when(t == line - 1)
        def _():
            go(z)

    steps = line * parts
    ahead = min(AHEAD, steps)
    for s in range(ahead):
        send_a(jnp.int32(s))

    def keep_own(w, _):
        start = pl.multiple_of((w * PLANE + p) * rows, rows)
        abuf[w, :, pl.ds(0, width)] = a_ref[pl.ds(start, rows), :]
        return 0

    lax.fori_loop(0, line, keep_own, 0)
    obuf[pl.ds(0, width), :] = o_ref[...]
    acc[...] = jnp.zeros_like(acc)
    for d in range(1, PLANE):
        o_copy(d).wait_recv()

    def product(w, j):
        for d in range(1, PLANE):
            a_copy(d, w, j).wait_recv()
        return jnp.dot(at(abuf, w, j)[...], obuf[...], precision=HIGHEST, preferred_element_type=jnp.float32)

    def use(w, j):
        block = at(full, w, j)[...]
        both = jnp.concatenate([block, at(abuf, w, j)[...]], axis=1)
        acc[...] += lax.dot_general(
            block, both, (((0,), (0,)), ((), ())), precision=HIGHEST, preferred_element_type=jnp.float32
        )

    def reduce_step(step, _):
        @pl.when(step + ahead < steps)
        def _():
            send_a(step + ahead)

        t, j = step // parts, step % parts

        def pass_on(way, w, inner):
            at(part, w, j)[...] = product(w, j)

            @pl.when(inner)
            def _():
                rs_copy(way, w, j).wait_recv()
                at(part, w, j)[...] += arrived[way, w, pl.ds(pl.multiple_of(j * sub, sub), sub), :]

            rs_copy(way, w, j).start()

        to_right = line - 1 - t > z

        @pl.when(jnp.logical_and(to_right, z < line // 2))
        def _():
            pass_on(0, line - 1 - t, has_left)

        @pl.when(jnp.logical_and(t < z, t < line - 1))
        def _():
            pass_on(1, t, has_right)

        @pl.when(jnp.logical_and(to_right, z >= line // 2))
        def _():
            pass_on(0, line - 1 - t, has_left)

        @pl.when(t == line - 1)
        def _():
            at(full, z, j)[...] = product(z, j)

            @pl.when(has_left)
            def _():
                rs_copy(0, z, j).wait_recv()
                at(full, z, j)[...] += arrived[0, z, pl.ds(pl.multiple_of(j * sub, sub), sub), :]

            @pl.when(has_right)
            def _():
                rs_copy(1, z, j).wait_recv()
                at(full, z, j)[...] += arrived[1, z, pl.ds(pl.multiple_of(j * sub, sub), sub), :]
                ag_copy(0, z, j).start()

            @pl.when(has_left)
            def _():
                ag_copy(1, z, j).start()

        return 0

    lax.fori_loop(0, steps, reduce_step, 0)
    y_out[...] = full[z]

    def own_step(j, _):
        use(z, j)
        return 0

    lax.fori_loop(0, parts, own_step, 0)

    def gather_step(step, _):
        t, j = step // parts + 1, step % parts

        @pl.when(t <= z)
        def _():
            w = z - t
            ag_copy(0, w, j).wait_recv()

            @pl.when(has_right)
            def _():
                ag_copy(0, w, j).start()

            use(w, j)

        @pl.when(z + t < line)
        def _():
            w = z + t
            ag_copy(1, w, j).wait_recv()

            @pl.when(has_left)
            def _():
                ag_copy(1, w, j).start()

            use(w, j)

        return 0

    lax.fori_loop(0, (line - 1) * parts, gather_step, 0)

    two = 2 * width
    core_copies = (
        remote(acc.at[:, pl.ds(0, rank)], from_core.at[:, pl.ds(0, rank)],
               fin_send.at[0], fin_recv.at[0], base + place[2]),
        remote(acc.at[:, pl.ds(rank + two, two)], from_core.at[:, pl.ds(rank, two)],
               fin_send.at[1], fin_recv.at[1], base + place[2]),
    )
    for copy in core_copies:
        copy.start()
    for copy in core_copies:
        copy.wait()
    acc[:, pl.ds(0, rank + two)] += from_core[...]
    y_copies = (
        remote(acc.at[:, pl.ds(0, rank)], from_y.at[:, pl.ds(0, rank)],
               fin_send.at[2], fin_recv.at[2], base + place[1]),
        remote(acc.at[:, pl.ds(rank + width, width)], from_y.at[:, pl.ds(rank, width)],
               fin_send.at[3], fin_recv.at[3], base + place[1]),
    )
    for copy in y_copies:
        copy.start()
    for copy in y_copies:
        copy.wait()
    g_out[...] = acc[:, pl.ds(0, rank)] + from_y[:, pl.ds(0, rank)]
    p_out[...] = acc[:, pl.ds(rank, width)] + from_y[:, pl.ds(rank, width)]

    for d in range(1, PLANE):
        o_copy(d).wait_send()

    def drain(step, _):
        w, j = step // parts, step % parts
        for d in range(1, PLANE):
            a_copy(d, w, j).wait_send()

        @pl.when(w != z)
        def _():
            rs_copy(0, w, j).wait_send()

        @pl.when(jnp.logical_and(has_right, w <= z))
        def _():
            ag_copy(0, w, j).wait_send()

        @pl.when(jnp.logical_and(has_left, w >= z))
        def _():
            ag_copy(1, w, j).wait_send()

        return 0

    lax.fori_loop(0, steps, drain, 0)


def exchange(n, samples, test_matrix):
    channels, width = samples.shape
    rank = test_matrix.shape[1]
    line = n // PLANE
    rows = channels // n
    sub = min(128, rows)
    parts = rows // sub
    f32 = jnp.float32
    dma = pltpu.SemaphoreType.DMA
    vmem = pl.BlockSpec(memory_space=pltpu.VMEM)
    return pl.pallas_call(
        functools.partial(exchange_kernel, line, parts, sub),
        out_shape=(
            jax.ShapeDtypeStruct((rows, rank), f32),
            jax.ShapeDtypeStruct((rank, rank), f32),
            jax.ShapeDtypeStruct((rank, width), f32),
        ),
        in_specs=[vmem] * 2,
        out_specs=(vmem,) * 3,
        scratch_shapes=[
            pltpu.VMEM((line, rows, PLANE * width), f32),
            pltpu.VMEM((PLANE * width, rank), f32),
            pltpu.VMEM((line, rows, rank), f32),
            pltpu.VMEM((2, line, rows, rank), f32),
            pltpu.VMEM((line, rows, rank), f32),
            pltpu.VMEM((rank, rank + PLANE * width), f32),
            pltpu.VMEM((rank, rank + 2 * width), f32),
            pltpu.VMEM((rank, rank + width), f32),
            dma((PLANE - 1, line, parts)),
            dma((PLANE - 1, line, parts)),
            dma((PLANE - 1,)),
            dma((PLANE - 1,)),
            dma((line, parts)),
            dma((2, line, parts)),
            dma((2, line, parts)),
            dma((line, parts)),
            dma((4,)),
            dma((4,)),
        ],
        compiler_params=pltpu.CompilerParams(
            collective_id=0, has_side_effects=True, vmem_limit_bytes=40 * 1024 * 1024
        ),
    )(samples, test_matrix)


def dot(a, b, contract=(1, 0)):
    return lax.dot_general(
        a, b, (((contract[0],), (contract[1],)), ((), ())), precision=HIGHEST, preferred_element_type=jnp.float32
    )


def inverse_factor(gram):
    n = gram.shape[0]
    blocks = n // 8
    row = lax.broadcasted_iota(jnp.int32, (8, n), 0)
    lane = lax.broadcasted_iota(jnp.int32, (8, n), 1)
    left = [gram[8 * i : 8 * i + 8, :] for i in range(blocks)]
    right = [jnp.where(lane == row + 8 * i, 1.0, 0.0) for i in range(blocks)]

    def spread(block, j):
        return jnp.broadcast_to(block[j : j + 1, :], (8, n))

    done = []
    for g in range(blocks):
        cols = {
            i: [jnp.broadcast_to(left[i][:, 8 * g + j : 8 * g + j + 1], (8, n)) for j in range(8)]
            for i in range(g, blocks)
        }
        scale = jnp.zeros((8, n), jnp.float32)
        for j in range(8):
            pivot = spread(cols[g][j], j)
            inverse = 1.0 / pivot
            scale = jnp.where(row == j, lax.rsqrt(pivot), scale)
            across = [spread(cols[g][j], l) for l in range(8)]
            left_row, right_row = spread(left[g], j), spread(right[g], j)
            for i in range(g, blocks):
                times = cols[i][j] * inverse
                if i == g:
                    times = jnp.where(row > j, times, 0.0)
                for l in range(j + 1, 8):
                    cols[i][l] = cols[i][l] - times * across[l]
                left[i] = left[i] - times * left_row
                right[i] = right[i] - times * right_row
        done.append(right[g] * scale)
    return jnp.concatenate(done, axis=0)


def inverse_of(gram):
    rank = gram.shape[0]
    if rank <= 128:
        return inverse_factor(gram)
    half = rank // 2
    first = inverse_of(gram[:half, :half])
    lower = dot(gram[half:, :half], first, (1, 1))
    second = inverse_of(gram[half:, half:] - dot(lower, lower, (1, 1)))
    corner = -dot(second, dot(lower, first))
    top = jnp.concatenate([first, jnp.zeros_like(first)], axis=1)
    return jnp.concatenate([top, jnp.concatenate([corner, second], axis=1)], axis=0)


def factor_kernel(root, y_ref, g_ref, p_ref, basis_ref, coordinates_ref):
    inverse = inverse_of(g_ref[...])
    basis_ref[...] = dot(y_ref[...], inverse, (1, 1)) * root
    coordinates_ref[...] = dot(inverse, p_ref[...])


def local(n, samples, test_matrix):
    channels = samples.shape[0]
    sketch, gram, projected = exchange(n, samples, test_matrix)
    vmem = pl.BlockSpec(memory_space=pltpu.VMEM)
    return pl.pallas_call(
        functools.partial(factor_kernel, float(channels) ** 0.5),
        out_shape=(
            jax.ShapeDtypeStruct(sketch.shape, jnp.float32),
            jax.ShapeDtypeStruct(projected.shape, jnp.float32),
        ),
        in_specs=[vmem] * 3,
        out_specs=(vmem,) * 2,
        compiler_params=pltpu.CompilerParams(vmem_limit_bytes=16 * 1024 * 1024),
    )(sketch, gram, projected)


def solution(mesh):
    placed = (P("groups", "tm"), P(("groups", "tm"), None))
    return jax.shard_map(
        functools.partial(local, mesh.shape["tm"]),
        mesh=mesh,
        in_specs=placed,
        out_specs=(P(("groups", "tm"), None), P("groups", "tm")),
        check_vma=False,
    )
```
